32 devices in a mesh: dp: 16 (over z, y, core), tensor: 2 (over x).
Axes of the slice: x: 2, y: 2, z: 4, core: 2. Of those that a mesh axis runs over, the one named last changes fastest.
Arguments:
- tokens: bfloat16 [16384, 1536], P(('dp', 'tensor')), may hold values from -6 to 6
- attn_gain: bfloat16 [1536], P('dp'), may hold values from 0.099609375 to 1.8984375
- ffn_gain: bfloat16 [1536], P('dp'), may hold values from 0.099609375 to 1.8984375
- router: bfloat16 [1536, 8], P('dp'), may hold values from -0.078125 to 0.078125
- w_query: bfloat16 [1536, 1536], P('dp', 'tensor'), may hold values from -0.15625 to 0.15625
- key_matrix: bfloat16 [1536, 256], P('dp', 'tensor'), may hold values from -0.15625 to 0.15625
- value_matrix: bfloat16 [1536, 256], P('dp', 'tensor'), may hold values from -0.15625 to 0.15625
- w_out_t: bfloat16 [1536, 1536], P('dp', 'tensor'), may hold values from -1.75 to 1.75
- w_gate: bfloat16 [8, 1536, 768], P(None, 'dp', 'tensor'), may hold values from -0.15625 to 0.15625
- w_up: bfloat16 [8, 1536, 768], P(None, 'dp', 'tensor'), may hold values from -0.15625 to 0.15625
- w_down_t: bfloat16 [8, 1536, 768], P(None, 'dp', 'tensor'), may hold values from -0.21875 to 0.21875
- lengths: int32 [16], P('dp'), may hold values from 513 to 1024, as said below
- routes: int32 [16384, 4], P('dp'), may hold values from 0 to 7, all different within a row
- priority: int32 [16384, 4], P('dp'), may hold values from 0 to 4095, as said below
- cotangent: bfloat16 [16384, 1536], P(('dp', 'tensor')), may hold values from -6 to 6
Outputs:
- block_out: bfloat16 [16384, 1536], P(('dp', 'tensor'))
- input_grad: float32 [16384, 1536], P(('dp', 'tensor'))
- attn_gain_grad: float32 [1536], P('dp')
- ffn_gain_grad: float32 [1536], P('dp')
- router_grad: float32 [1536, 8], P('dp')
- w_query_grad: float32 [1536, 1536], P('dp', 'tensor')
- w_key_grad: float32 [1536, 256], P('dp', 'tensor')
- w_value_grad: float32 [1536, 256], P('dp', 'tensor')
- w_out_t_grad: float32 [1536, 1536], P('dp', 'tensor')
- w_gate_grad: float32 [8, 1536, 768], P(None, 'dp', 'tensor')
- w_up_grad: float32 [8, 1536, 768], P(None, 'dp', 'tensor')
- w_down_t_grad: float32 [8, 1536, 768], P(None, 'dp', 'tensor')
The draws below stay inside these ranges and needn't reach their ends.
Inputs may be any that keep to these rules, and one draw needn't show every extreme that they name: `lengths`: every length is over half of 1024; some sequence has exactly 1024. `priority`: within each group of 1024 rows the entries are a permutation of 0 to 4095.
All inputs are finite; a program needn't handle non-finite values.
Results may differ from the reference program's by a relative error of at most 0.022.
Values may be sent and summed in bfloat16 or wider, within the bound.
A program may use at most 320 MiB of HBM per device.

```python
import jax
import jax.numpy as jnp
from jax import lax

MODEL_WIDTH = 1536
QUERY_HEADS = 12
KEY_VALUE_HEADS = 2
HEAD_SIZE = 128
FF = 768
TOP = 4
EXPERTS = 8
SLOT_POSITIONS = 1024
SEQS = 1
GROUP = 1024
TOKENS = 16384
SEQUENCES = 16
CAP = 512


def draw_lengths(key, part):
    key = jax.random.fold_in(key, 11)
    base_len = jax.random.randint(key, (SEQUENCES,), SLOT_POSITIONS // 2 + 1, SLOT_POSITIONS + 1, dtype=jnp.int32)
    chosen_one = jax.random.randint(jax.random.fold_in(key, 1), (), 0, SEQUENCES, dtype=jnp.int32)
    return jnp.where(jnp.arange(SEQUENCES, dtype=jnp.int32) == chosen_one, SLOT_POSITIONS, base_len).astype(jnp.int32)


def draw_priority(key, part):
    key = jax.random.fold_in(key, 23)
    group_keys = jax.random.split(key, TOKENS // GROUP)
    orders = jax.vmap(lambda one_key: jax.random.permutation(one_key, GROUP * TOP))(group_keys)
    return orders.reshape(TOKENS, TOP).astype(jnp.int32)


def steps_of(own_key, dims, cuts, low, largest):
    loudness, own = 1.0, jax.random.fold_in(own_key, 6)
    for dim, blocks in cuts:
        steps = jnp.exp(jax.random.uniform(jax.random.fold_in(own, dim), (blocks,), jnp.float32, low / len(cuts), largest / len(cuts)))
        loudness = loudness * jnp.repeat(steps, dims[dim] // blocks).reshape([-1 if axis == dim else 1 for axis in range(len(dims))])
    return loudness


def choose_distinct(stream_key, rows, number_of, top, lift):
    order = jax.random.permutation(jax.random.fold_in(stream_key, 1), number_of)
    boost = order
    for power in range(3):
        boost = boost * boost // number_of
    boost = boost * lift // number_of
    chance = jax.random.randint(jax.random.fold_in(stream_key, 2), (rows, number_of), 0, 4096) + boost
    sure = jax.random.permutation(jax.random.fold_in(stream_key, 3), rows)[jnp.arange(number_of) % rows]
    chance = jnp.where(jnp.arange(rows)[:, None] == sure[None, :], 1 << 14, chance)
    score = chance * number_of + jnp.arange(number_of)
    return lax.top_k(score.astype(jnp.int32), top)[1].astype(jnp.int32)


def noise(stream_key, extent, width, reach, cuts=(), kind=jnp.bfloat16):
    entries = width * jax.random.normal(stream_key, extent, jnp.float32)
    if cuts:
        entries = entries * steps_of(stream_key, extent, cuts, -0.22, 0.18)
    return jnp.clip(entries, -reach, reach).astype(kind)


def setup_inputs(seed: int = 0) -> dict:
    key_list = jax.random.split(jax.random.key(seed), 16)
    return {
        "tokens": noise(key_list[0], (TOKENS, MODEL_WIDTH), 1.0, 6.0, ((0, 32),)),
        "attn_gain": jnp.clip(1.0 + 0.18 * jax.random.normal(key_list[1], (MODEL_WIDTH,), jnp.float32), 0.099609375, 1.8984375).astype(jnp.bfloat16),
        "ffn_gain": jnp.clip(1.0 + 0.18 * jax.random.normal(key_list[2], (MODEL_WIDTH,), jnp.float32), 0.099609375, 1.8984375).astype(jnp.bfloat16),
        "router": noise(key_list[3], (MODEL_WIDTH, EXPERTS), (4 * MODEL_WIDTH) ** -0.5, 0.078125, ((0, 16),)),
        "w_query": noise(key_list[4], (MODEL_WIDTH, QUERY_HEADS * HEAD_SIZE), MODEL_WIDTH ** -0.5, 0.15625, ((0, 16), (1, 2))),
        "key_matrix": noise(key_list[5], (MODEL_WIDTH, KEY_VALUE_HEADS * HEAD_SIZE), MODEL_WIDTH ** -0.5, 0.15625, ((0, 16), (1, 2))),
        "value_matrix": noise(key_list[6], (MODEL_WIDTH, KEY_VALUE_HEADS * HEAD_SIZE), MODEL_WIDTH ** -0.5, 0.15625, ((0, 16), (1, 2))),
        "w_out_t": noise(key_list[7], (MODEL_WIDTH, QUERY_HEADS * HEAD_SIZE), (QUERY_HEADS * HEAD_SIZE // 128) ** -0.5, 1.75, ((0, 16), (1, 2))),
        "w_gate": noise(key_list[8], (EXPERTS, MODEL_WIDTH, FF), MODEL_WIDTH ** -0.5, 0.15625, ((1, 16), (2, 2))),
        "w_up": noise(key_list[9], (EXPERTS, MODEL_WIDTH, FF), MODEL_WIDTH ** -0.5, 0.15625, ((1, 16), (2, 2))),
        "w_down_t": noise(key_list[10], (EXPERTS, MODEL_WIDTH, FF), FF ** -0.5, 0.21875, ((1, 16), (2, 2))),
        "lengths": draw_lengths(jax.random.fold_in(key_list[15], 71), 0),
        "routes": choose_distinct(key_list[12], TOKENS, EXPERTS, TOP, 4096),
        "priority": draw_priority(jax.random.fold_in(key_list[15], 71), 0),
        "cotangent": noise(key_list[14], (TOKENS, MODEL_WIDTH), 1.0, 6.0, ((0, 32),)),
    }


EPSILON = 1e-06
ROPE_BASE = 10000.0
MASKED = -1e+30
HIGHEST_ACCURACY = lax.Precision.HIGHEST

@jax.custom_vjp
def low(v):
    return lax.optimization_barrier(v.astype(jnp.bfloat16)).astype(jnp.float32)

@jax.custom_vjp
def low_back(v):
    return v

def low_keep(v):
    return (low(v), None)

def low_pass(kept, grad):
    return (grad,)

def back_keep(v):
    return (v, None)

def back_low(kept, grad):
    return (low(grad),)
low.defvjp(low_keep, low_pass)
low_back.defvjp(back_keep, back_low)

def route_slots(routes, priority, valid_rows, capacity):
    local_tokens = routes.shape[0]
    top_k = routes.shape[1]
    pair_count = local_tokens * top_k
    experts_flat = routes.reshape(pair_count)
    ranks_flat = priority.reshape(pair_count)
    live_pairs = jnp.repeat(valid_rows.astype(jnp.int32), top_k)
    pair_ids = jnp.arange(pair_count, dtype=jnp.int32)
    ordering = jnp.zeros((pair_count,), jnp.int32).at[ranks_flat].set(pair_ids)
    columns = jnp.arange(EXPERTS, dtype=jnp.int32)
    onehot = (experts_flat[ordering][:, None] == columns[None, :]).astype(jnp.int32) * live_pairs[ordering][:, None]
    earlier = jnp.cumsum(onehot, axis=0, dtype=jnp.int32) - onehot
    rank_sorted = lax.optimization_barrier(jnp.sum(earlier * onehot, axis=1, dtype=jnp.int32))
    place_rank = rank_sorted[ranks_flat]
    keeping = (live_pairs > 0) & (place_rank < capacity)
    slot_ids = jnp.where(keeping, experts_flat * capacity + place_rank, EXPERTS * capacity).astype(jnp.int32)
    slot_table = jnp.full((EXPERTS * capacity + 1,), pair_count, jnp.int32).at[slot_ids].set(pair_ids)
    return (keeping.reshape(local_tokens, top_k), slot_ids.reshape(local_tokens, top_k), slot_table[:EXPERTS * capacity])

def rope_tables(places):
    half_dim = HEAD_SIZE // 2
    frequency = ROPE_BASE ** (-jnp.arange(half_dim, dtype=jnp.float32) / half_dim)
    angles = places.astype(jnp.float32)[:, None] * frequency[None, :]
    return (jnp.cos(angles)[:, None, :], jnp.sin(angles)[:, None, :])

def apply_rotary(values, cosine_lookup, sine_lookup):
    half_dim = values.shape[-1] // 2
    first_half = values[..., :half_dim]
    second_half = values[..., half_dim:]
    return jnp.concatenate([first_half * cosine_lookup - second_half * sine_lookup, second_half * cosine_lookup + first_half * sine_lookup], axis=-1)

def rms_norm(values, gain_vec):
    return values * lax.rsqrt(lax.optimization_barrier(jnp.mean(values * values, axis=1, keepdims=True)) + EPSILON) * gain_vec

def attention(query_rows, every_key, every_value, valid_rows):
    sequence_count = query_rows.shape[0] // SLOT_POSITIONS
    heads_per_group = QUERY_HEADS // KEY_VALUE_HEADS
    query_tiles = query_rows.reshape(sequence_count, SLOT_POSITIONS, KEY_VALUE_HEADS, heads_per_group, HEAD_SIZE)
    key_tiles = every_key.reshape(sequence_count, SLOT_POSITIONS, KEY_VALUE_HEADS, HEAD_SIZE)
    value_tiles = every_value.reshape(sequence_count, SLOT_POSITIONS, KEY_VALUE_HEADS, HEAD_SIZE)
    scores = jnp.einsum('sqgrd,skgd->sgrqk', query_tiles, key_tiles, precision=HIGHEST_ACCURACY)
    scores = low_back(scores * HEAD_SIZE ** (-0.5))
    places = jnp.arange(SLOT_POSITIONS, dtype=jnp.int32)
    allowed = (places[None, :] <= places[:, None])[None, None, None] & valid_rows.reshape(sequence_count, 1, 1, 1, SLOT_POSITIONS)
    scores = jnp.where(allowed, scores, MASKED)
    prob_low = low(jax.nn.softmax(scores, axis=-1))
    heads_out = jnp.einsum('sgrqk,skgd->sqgrd', prob_low, value_tiles, precision=HIGHEST_ACCURACY)
    return heads_out.reshape(sequence_count * SLOT_POSITIONS, QUERY_HEADS * HEAD_SIZE)

def layer_forward(inputs, attn_gain, ffn_gain, router, w_query, key_matrix, value_matrix, w_out_t, w_gate, w_up, w_down_t, valid_rows, valid_f, cosine_lookup, sine_lookup, routes, keep_f, slot_ids, slot_table):
    local_tokens = inputs.shape[0]
    normed_input = low(rms_norm(inputs, attn_gain))
    query_rows = low(apply_rotary(low_back(jnp.dot(normed_input, w_query, precision=HIGHEST_ACCURACY)).reshape(local_tokens, QUERY_HEADS, HEAD_SIZE), cosine_lookup, sine_lookup))
    every_key = low(apply_rotary(low_back(jnp.dot(normed_input, key_matrix, precision=HIGHEST_ACCURACY)).reshape(local_tokens, KEY_VALUE_HEADS, HEAD_SIZE), cosine_lookup, sine_lookup))
    every_value = low_back(low(jnp.dot(normed_input, value_matrix, precision=HIGHEST_ACCURACY))).reshape(local_tokens, KEY_VALUE_HEADS, HEAD_SIZE)
    heads_out = low_back(low(attention(query_rows, every_key, every_value, valid_rows)))
    branch = low_back(jnp.dot(heads_out, w_out_t.T, precision=HIGHEST_ACCURACY))
    middle = inputs + branch
    normed_ffn = low(rms_norm(middle, ffn_gain))
    logits = low_back(jnp.dot(normed_ffn, router, precision=HIGHEST_ACCURACY))
    chosen = jnp.take_along_axis(logits, routes, axis=1)
    gates = jax.nn.softmax(chosen, axis=1) * keep_f
    filled = slot_table < local_tokens * TOP
    token_rows = jnp.minimum(slot_table // TOP, local_tokens - 1)
    expert_in = jnp.where(filled[:, None], normed_ffn[token_rows], 0.0).reshape(EXPERTS, CAP, MODEL_WIDTH)
    gate_pre = low_back(jnp.einsum('ecd,edf->ecf', expert_in, w_gate, precision=HIGHEST_ACCURACY))
    up_pre = low_back(jnp.einsum('ecd,edf->ecf', expert_in, w_up, precision=HIGHEST_ACCURACY))
    hidden = low(jax.nn.silu(gate_pre) * up_pre)
    expert_out = low_back(jnp.einsum('ecf,edf->ecd', hidden, w_down_t, precision=HIGHEST_ACCURACY)).reshape(EXPERTS * CAP, MODEL_WIDTH)
    picked = expert_out[jnp.minimum(slot_ids, EXPERTS * CAP - 1)]
    ffn_sum = low_back(lax.optimization_barrier(jnp.sum(gates[:, :, None] * picked, axis=1)))
    return valid_f[:, None] * (middle + ffn_sum)

def reference(tokens, attn_gain, ffn_gain, router, w_query, key_matrix, value_matrix, w_out_t, w_gate, w_up, w_down_t, lengths, routes, priority, cotangent):
    weights = tuple((w.astype(jnp.float32) for w in (attn_gain, ffn_gain, router, w_query, key_matrix, value_matrix, w_out_t, w_gate, w_up, w_down_t)))
    groups = TOKENS // GROUP
    places = jnp.arange(GROUP, dtype=jnp.int32) % SLOT_POSITIONS
    seq_of = jnp.arange(GROUP, dtype=jnp.int32) // SLOT_POSITIONS
    cosine_lookup, sine_lookup = rope_tables(places)

    def one_group(totals, one_item):
        inputs, group_lengths, group_routes, group_priority, group_cot = one_item
        valid_rows = places < group_lengths[seq_of]
        valid_f = valid_rows.astype(jnp.float32)
        keeping, slot_ids, slot_table = route_slots(group_routes, group_priority, valid_rows, CAP)
        keep_f = keeping.astype(jnp.float32)

        def forward(inputs, *parameters):
            return layer_forward(inputs, *parameters, valid_rows, valid_f, cosine_lookup, sine_lookup, group_routes, keep_f, slot_ids, slot_table)
        output, pullback = jax.vjp(forward, inputs, *weights)
        gradients = pullback(group_cot)
        totals = tuple((total + grad for total, grad in zip(totals, gradients[1:])))
        return (totals, (output.astype(jnp.bfloat16), gradients[0]))
    initial = tuple((jnp.zeros_like(w) for w in weights))
    scanned = (tokens.astype(jnp.float32).reshape(groups, GROUP, MODEL_WIDTH), lengths.reshape(groups, SEQS), routes.reshape(groups, GROUP, TOP), priority.reshape(groups, GROUP, TOP), cotangent.astype(jnp.float32).reshape(groups, GROUP, MODEL_WIDTH))
    totals, (outputs, input_grads) = lax.scan(one_group, initial, scanned)
    return (outputs.reshape(TOKENS, MODEL_WIDTH), input_grads.reshape(TOKENS, MODEL_WIDTH), totals[0], totals[1], totals[2], totals[3], totals[4], totals[5], totals[6], totals[7], totals[8], totals[9])
```

```python
import functools

import jax
import jax.numpy as jnp
from jax import lax
from jax.experimental import pallas as pl
from jax.experimental.pallas import tpu as pltpu
from jax.sharding import PartitionSpec as P

WIDTH = 1536
HEADS = 12
KV_HEADS = 2
HEAD = 128
FF = 768
TOP = 4
EXPERTS = 8
GROUP = 1024
CAP = 512
EPSILON = 1e-06
ROPE_BASE = 10000.0
F32 = jnp.float32
BF16 = jnp.bfloat16
LANES = 128
ROWS = 256
SCALE = HEAD ** (-0.5)
VMEM_LIMIT = 60 * 1024 * 1024


def dot(left, right):
    return jnp.dot(left, right, preferred_element_type=F32)


def dot_nt(left, right):
    return lax.dot_general(left, right, (((1,), (1,)), ((), ())), preferred_element_type=F32)


def params(**kw):
    return pltpu.CompilerParams(vmem_limit_bytes=VMEM_LIMIT, **kw)


def whole(shape):
    zeros = (0,) * len(shape)
    return pl.BlockSpec(shape, lambda *_: zeros)


def once(shape):
    zeros = (0,) * len(shape)
    return pl.BlockSpec(shape, lambda *_: zeros, pipeline_mode=pl.Buffered(1))


def route_kernel(length_ref, routes_ref, priority_ref, member_ref, keep_ref):
    expert = lax.broadcasted_iota(jnp.int32, (EXPERTS, GROUP), 0)
    place = lax.broadcasted_iota(jnp.int32, (EXPERTS, GROUP), 1)
    order = jnp.full((EXPERTS, GROUP), 1 << 20, jnp.int32)
    for j in range(TOP):
        order = jnp.where(routes_ref[j : j + 1, :] == expert, priority_ref[j : j + 1, :], order)
    member = order < (1 << 19)
    order = jnp.where(place < length_ref[0], order, 1 << 20)
    bound = jnp.zeros((EXPERTS, 1), jnp.int32)
    for bit in range(12, -1, -1):
        trial = bound + (1 << bit)
        count = jnp.sum((order < trial).astype(F32), axis=1, keepdims=True)
        bound = jnp.where(count <= CAP, trial, bound)
    member_ref[...] = member.astype(F32)
    keep_ref[...] = (order < bound).astype(F32)


def route(length, routes, priority):
    return pl.pallas_call(
        route_kernel,
        name="route",
        out_shape=(jax.ShapeDtypeStruct((EXPERTS, GROUP), F32),) * 2,
        in_specs=[
            pl.BlockSpec(memory_space=pltpu.SMEM),
            pl.BlockSpec(memory_space=pltpu.VMEM),
            pl.BlockSpec(memory_space=pltpu.VMEM),
        ],
        out_specs=(pl.BlockSpec(memory_space=pltpu.VMEM),) * 2,
    )(length, routes.T, priority.T)


def rope(v, cos, sin):
    return v * cos + pltpu.roll(v, HEAD // 2, 1) * sin


def qkv_kernel(x_ref, gain_ref, w_ref, cos_ref, sin_ref, xnt_ref, q_ref, k_ref, v_ref):
    x = x_ref[...].astype(F32)
    scale = lax.rsqrt(jnp.mean(x * x, axis=1, keepdims=True) + EPSILON)
    xn = (x * scale * gain_ref[...]).astype(BF16)
    xnt_ref[...] = xn.T
    cos, sin = cos_ref[...], sin_ref[...]
    q_width = q_ref.shape[1]
    out = dot(xn, w_ref[:, : q_width + 2 * HEAD])
    for h in range(q_width // HEAD):
        cols = slice(h * HEAD, (h + 1) * HEAD)
        q_ref[:, cols] = rope(out[:, cols], cos, sin).astype(BF16)
    k_ref[...] = rope(out[:, q_width : q_width + HEAD], cos, sin).astype(BF16)
    v_ref[...] = out[:, q_width + HEAD :].astype(BF16)


def qkv(x, gain, weights, cos, sin, q_width):
    rows = lambda width: pl.BlockSpec((ROWS, width), lambda i: (i, 0))
    return pl.pallas_call(
        qkv_kernel,
        name="qkv",
        grid=(GROUP // ROWS,),
        out_shape=(
            jax.ShapeDtypeStruct((WIDTH, GROUP), BF16),
            jax.ShapeDtypeStruct((GROUP, q_width), BF16),
            jax.ShapeDtypeStruct((GROUP, HEAD), BF16),
            jax.ShapeDtypeStruct((GROUP, HEAD), BF16),
        ),
        in_specs=[
            rows(WIDTH),
            whole((1, WIDTH)),
            whole(weights.shape),
            rows(HEAD),
            rows(HEAD),
        ],
        out_specs=(
            pl.BlockSpec((WIDTH, ROWS), lambda i: (0, i)),
            rows(q_width),
            rows(HEAD),
            rows(HEAD),
        ),
        compiler_params=params(),
    )(x, gain, weights, cos, sin)


def scores_t(k, q, first_row, length):
    s = dot_nt(k, q) * SCALE
    key = lax.broadcasted_iota(jnp.int32, s.shape, 0)
    query = lax.broadcasted_iota(jnp.int32, (1, s.shape[1]), 1) + first_row
    return jnp.where(key < jnp.minimum(query + 1, length), s, -1e30)


def attend_kernel(half, length_ref, q_ref, k_ref, v_ref, o_ref, lse_ref):
    length = length_ref[0]
    vt = v_ref[...].T
    heads = q_ref.shape[1] // HEAD
    for block in range(q_ref.shape[0] // ROWS):
        first = half * q_ref.shape[0] + block * ROWS
        keys = first + ROWS
        rows = slice(block * ROWS, (block + 1) * ROWS)
        for h in range(heads):
            cols = slice(h * HEAD, (h + 1) * HEAD)
            s = scores_t(k_ref[:keys, :], q_ref[rows, cols], first, length)
            peak = jnp.max(s, axis=0, keepdims=True)
            e = jnp.exp(s - peak)
            total = jnp.sum(e, axis=0, keepdims=True)
            p = (e * (1.0 / total)).astype(BF16)
            ot = dot(vt[:, :keys], p)
            o_ref[rows, cols] = ot.T.astype(BF16)
            lse_ref[h : h + 1, rows] = peak + jnp.log(total)


def attend(half, halves, length, q, k, v):
    count = GROUP // halves
    q_width = q.shape[1]
    return pl.pallas_call(
        functools.partial(attend_kernel, half),
        name="attend",
        grid=(1,),
        out_shape=(
            jax.ShapeDtypeStruct((count, q_width), BF16),
            jax.ShapeDtypeStruct((8, count), F32),
        ),
        in_specs=[
            pl.BlockSpec(memory_space=pltpu.SMEM),
            pl.BlockSpec((count, q_width), lambda i: (half, 0)),
            whole((GROUP, HEAD)),
            whole((GROUP, HEAD)),
        ],
        out_specs=(whole((count, q_width)), whole((8, count))),
        compiler_params=params(),
    )(length, q, k, v)


def attend_back_kernel(
    length_ref, g_ref, wo_ref, q_ref, k_ref, v_ref, lse_ref, cos_ref, sin_ref, out_ref, do_ref
):
    length = length_ref[0]
    heads = q_ref.shape[1] // HEAD
    width = q_ref.shape[1]
    for block in range(GROUP // ROWS):
        rows = slice(block * ROWS, (block + 1) * ROWS)
        do_ref[rows, :] = dot(g_ref[rows, :], wo_ref[:, :width]).astype(BF16)
    kt = k_ref[...].T
    dk = [jnp.zeros((ROWS, HEAD), F32) for _ in range(GROUP // ROWS)]
    dv = [jnp.zeros((ROWS, HEAD), F32) for _ in range(GROUP // ROWS)]
    for block in range(GROUP // ROWS):
        first = block * ROWS
        keys = first + ROWS
        rows = slice(first, keys)
        cos, sin = cos_ref[rows, :], sin_ref[rows, :]
        dk_sum = jnp.zeros((keys, HEAD), F32)
        dv_sum = jnp.zeros((keys, HEAD), F32)
        for h in range(heads):
            cols = slice(h * HEAD, (h + 1) * HEAD)
            q, do = q_ref[rows, cols], do_ref[rows, cols]
            s = scores_t(k_ref[:keys, :], q, first, length)
            p = jnp.exp(s - lse_ref[h : h + 1, rows])
            dp = dot_nt(v_ref[:keys, :], do)
            inner = jnp.sum(p * dp, axis=0, keepdims=True)
            ds = (p * (dp - inner)).astype(BF16)
            dv_sum += dot(p.astype(BF16), do)
            dk_sum += dot(ds, q)
            dq = dot(kt[:, :keys], ds).T * SCALE
            out_ref[rows, cols] = rope(dq, cos, -sin).astype(BF16)
        for j in range(block + 1):
            part = slice(j * ROWS, (j + 1) * ROWS)
            dk[j] += dk_sum[part]
            dv[j] += dv_sum[part]
    for block in range(GROUP // ROWS):
        rows = slice(block * ROWS, (block + 1) * ROWS)
        out_ref[rows, width : width + HEAD] = rope(
            dk[block] * SCALE, cos_ref[rows, :], -sin_ref[rows, :]
        ).astype(BF16)
        out_ref[rows, width + HEAD :] = dv[block].astype(BF16)


def attend_back(length, grad, wo, q, k, v, lse, cos, sin):
    q_width = q.shape[1]
    return pl.pallas_call(
        attend_back_kernel,
        name="attend_back",
        grid=(1,),
        out_shape=jax.ShapeDtypeStruct((GROUP, q_width + 2 * HEAD), BF16),
        in_specs=[
            pl.BlockSpec(memory_space=pltpu.SMEM),
            whole((GROUP, WIDTH)),
            whole(wo.shape),
            whole((GROUP, q_width)),
            whole((GROUP, HEAD)),
            whole((GROUP, HEAD)),
            whole((8, GROUP)),
            whole((GROUP, HEAD)),
            whole((GROUP, HEAD)),
        ],
        out_specs=whole((GROUP, q_width + 2 * HEAD)),
        scratch_shapes=[pltpu.VMEM((GROUP, q_width), BF16)],
        compiler_params=params(),
    )(length, grad, wo, q, k, v, lse, cos, sin)


def out_kernel(x_ref, oa_ref, ob_ref, wo_ref, gain_ref, r_ref, member_ref, keep_ref,
               h_ref, u_ref, ut_ref, gate_ref, weight_ref):
    width = oa_ref.shape[1]
    h = (
        dot_nt(oa_ref[...], wo_ref[:, :width]) + dot_nt(ob_ref[...], wo_ref[:, width:])
    ) + x_ref[...].astype(F32)
    h_ref[...] = h
    scale = lax.rsqrt(jnp.mean(h * h, axis=1, keepdims=True) + EPSILON)
    u = (h * scale * gain_ref[...]).astype(BF16)
    u_ref[...] = u
    ut_ref[...] = u.T
    z = dot(u, r_ref[...])
    member = member_ref[...] > 0
    peak = jnp.max(jnp.where(member, z, -1e30), axis=1, keepdims=True)
    e = jnp.where(member, jnp.exp(jnp.where(member, z - peak, 0.0)), 0.0)
    gate = e / jnp.sum(e, axis=1, keepdims=True)
    gate_ref[...] = gate
    weight_ref[...] = gate * keep_ref[...]


def out_project(half, halves, x, oa, ob, wo, gain, router, member, keep):
    count = GROUP // halves
    blocks = count // ROWS
    first = half * blocks
    local = lambda width: pl.BlockSpec((ROWS, width), lambda i: (i, 0))
    full = lambda width: pl.BlockSpec((ROWS, width), lambda i: (i + first, 0))
    return pl.pallas_call(
        out_kernel,
        name="out_project",
        grid=(blocks,),
        out_shape=(
            jax.ShapeDtypeStruct((count, WIDTH), F32),
            jax.ShapeDtypeStruct((count, WIDTH), BF16),
            jax.ShapeDtypeStruct((WIDTH, count), BF16),
            jax.ShapeDtypeStruct((count, LANES), F32),
            jax.ShapeDtypeStruct((count, LANES), F32),
        ),
        in_specs=[
            full(WIDTH),
            local(oa.shape[1]),
            local(ob.shape[1]),
            whole(wo.shape),
            whole((1, WIDTH)),
            whole((WIDTH, LANES)),
            full(LANES),
            full(LANES),
        ],
        out_specs=(
            local(WIDTH),
            local(WIDTH),
            pl.BlockSpec((WIDTH, ROWS), lambda i: (0, i)),
            local(LANES),
            local(LANES),
        ),
        compiler_params=params(),
    )(x, oa, ob, wo, gain, router, member, keep)


def experts_kernel(first_pair, chained, *refs):
    if chained:
        u_ref, g_ref, ut_ref, gt_ref, w_ref, weight_ref, f_in, du_in, dg_in = refs[:9]
        rest = refs[9:]
    else:
        u_ref, g_ref, ut_ref, gt_ref, w_ref, weight_ref = refs[:6]
        rest = refs[6:]
    dw_ref, f_ref, du_ref, dg_ref, f_acc, du_acc, dg_acc, dab, wh = rest
    pair, step = pl.program_id(0), pl.program_id(1)
    part = w_ref.shape[2] // 6
    blocks = GROUP // ROWS

    @pl.when(step < blocks)
    def _():
        rows = pl.ds(pl.multiple_of(step * ROWS, ROWS), ROWS)
        ab = dot(u_ref[...], w_ref[0, :, : 4 * part])
        d = dot(g_ref[...], w_ref[0, :, 4 * part :])
        lane = lax.broadcasted_iota(jnp.int32, (ROWS, LANES), 1)
        weights = weight_ref[...]
        fresh = pair == 0
        if chained:
            dg = jnp.where(fresh, dg_in[...], dg_acc[rows, :])
        else:
            dg = jnp.where(fresh, 0.0, dg_acc[rows, :])
        for i in range(2):
            mine = lane == 2 * (first_pair + pair) + i
            w = jnp.sum(jnp.where(mine, weights, 0.0), axis=1, keepdims=True)
            a = ab[:, 2 * i * part : (2 * i + 1) * part]
            b = ab[:, (2 * i + 1) * part : (2 * i + 2) * part]
            dh = d[:, i * part : (i + 1) * part]
            s = 1.0 / (1.0 + jnp.exp(-a))
            act = a * s
            hid = (act * b).astype(BF16).astype(F32)
            dg += jnp.where(mine, jnp.sum(hid * dh, axis=1, keepdims=True), 0.0)
            wh[rows, i * part : (i + 1) * part] = (w * hid).astype(BF16)
            dh = dh * w
            dab[rows, 2 * i * part : (2 * i + 1) * part] = (
                dh * b * (s * (1.0 + a * (1.0 - s)))
            ).astype(BF16)
            dab[rows, (2 * i + 1) * part : (2 * i + 2) * part] = (dh * act).astype(BF16)
        dg_acc[rows, :] = dg
        dg_ref[...] = dg
        f = dot_nt(wh[rows, :], w_ref[0, :, 4 * part :])
        du = dot_nt(dab[rows, :], w_ref[0, :, : 4 * part])
        if chained:
            f += jnp.where(fresh, f_in[...].astype(F32), f_acc[rows, :])
            du += jnp.where(fresh, du_in[...].astype(F32), du_acc[rows, :])
        else:
            f += jnp.where(fresh, 0.0, f_acc[rows, :])
            du += jnp.where(fresh, 0.0, du_acc[rows, :])
        f_acc[rows, :] = f
        du_acc[rows, :] = du
        f_ref[...] = f.astype(BF16)
        du_ref[...] = du.astype(BF16)

    for tile in range(3):

        @pl.when(step == blocks + tile)
        def _():
            if tile < 2:
                out = dot(ut_ref[...], dab[:, 2 * tile * part : (2 * tile + 2) * part])
            else:
                out = dot(gt_ref[...], wh[...])
            dw_ref[0] = out.astype(BF16)


def experts(first_pair, u, g, ut, gt, weights, gates, carried=None):
    pairs, _, cols = weights.shape
    part = cols // 6
    blocks = GROUP // ROWS
    chained = carried is not None
    row = lambda width: pl.BlockSpec((ROWS, width), lambda p, s: (jnp.minimum(s, blocks - 1), 0))
    begin = lambda width: pl.BlockSpec(
        (ROWS, width), lambda p, s: (jnp.where(p == 0, jnp.minimum(s, blocks - 1), blocks - 1), 0)
    )
    finish = lambda width: pl.BlockSpec(
        (ROWS, width), lambda p, s: (jnp.where(p == pairs - 1, jnp.minimum(s, blocks - 1), 0), 0)
    )
    in_specs = [
        row(WIDTH),
        row(WIDTH),
        once((WIDTH, GROUP)),
        once((WIDTH, GROUP)),
        pl.BlockSpec((1, WIDTH, cols), lambda p, s: (p, 0, 0)),
        row(LANES),
    ]
    operands = [u, g, ut, gt, weights, gates]
    if chained:
        in_specs += [begin(WIDTH), begin(WIDTH), begin(LANES)]
        operands += list(carried)
    return pl.pallas_call(
        functools.partial(experts_kernel, first_pair, chained),
        name="experts",
        grid=(pairs, blocks + 3),
        out_shape=(
            jax.ShapeDtypeStruct(weights.shape, BF16),
            jax.ShapeDtypeStruct((GROUP, WIDTH), BF16),
            jax.ShapeDtypeStruct((GROUP, WIDTH), BF16),
            jax.ShapeDtypeStruct((GROUP, LANES), F32),
        ),
        in_specs=in_specs,
        out_specs=(
            pl.BlockSpec((1, WIDTH, 2 * part), lambda p, s: (p, 0, jnp.maximum(s - blocks, 0))),
            finish(WIDTH),
            finish(WIDTH),
            finish(LANES),
        ),
        scratch_shapes=[
            pltpu.VMEM((GROUP, WIDTH), F32),
            pltpu.VMEM((GROUP, WIDTH), F32),
            pltpu.VMEM((GROUP, LANES), F32),
            pltpu.VMEM((GROUP, 4 * part), BF16),
            pltpu.VMEM((GROUP, 2 * part), BF16),
        ],
        compiler_params=params(),
    )(*operands)


def gates_back_kernel(mine_ref, other_ref, gate_ref, keep_ref, ut_ref, dz_ref, router_ref):
    dg = (mine_ref[...] + other_ref[...]) * keep_ref[...]
    gate = gate_ref[...]
    dz = (gate * (dg - jnp.sum(gate * dg, axis=1, keepdims=True))).astype(BF16)
    dz_ref[...] = dz
    router_ref[...] = dot(ut_ref[...], dz)


def gates_back(mine, other, gate, keep, ut):
    return pl.pallas_call(
        gates_back_kernel,
        name="gates_back",
        out_shape=(
            jax.ShapeDtypeStruct((GROUP, LANES), BF16),
            jax.ShapeDtypeStruct((WIDTH, LANES), F32),
        ),
        compiler_params=params(),
    )(mine, other, gate, keep, ut)


def middle_kernel(h_ref, mine_ref, other_ref, dz_ref, r_ref, g_ref, gain_ref,
                  dh_ref, low_ref, lowt_ref, gain_grad_ref):
    h = h_ref[...]
    du = mine_ref[...].astype(F32) + other_ref[...].astype(F32) + dot_nt(dz_ref[...], r_ref[...])
    scale = lax.rsqrt(jnp.mean(h * h, axis=1, keepdims=True) + EPSILON)
    gain = gain_ref[...]
    inner = jnp.mean(du * gain * h, axis=1, keepdims=True)
    dh = g_ref[...].astype(F32) + scale * gain * du - h * (scale * scale * scale) * inner
    dh_ref[...] = dh
    low = dh.astype(BF16)
    low_ref[...] = low
    lowt_ref[...] = low.T
    part = jnp.sum(du * h * scale, axis=0, keepdims=True)
    first = pl.program_id(0) == 0
    gain_grad_ref[...] = jnp.where(first, 0.0, gain_grad_ref[...]) + part


def middle_back(h, mine, other, dz, router, g, gain):
    rows = lambda width: pl.BlockSpec((ROWS, width), lambda i: (i, 0))
    return pl.pallas_call(
        middle_kernel,
        name="middle_back",
        grid=(GROUP // ROWS,),
        out_shape=(
            jax.ShapeDtypeStruct((GROUP, WIDTH), F32),
            jax.ShapeDtypeStruct((GROUP, WIDTH), BF16),
            jax.ShapeDtypeStruct((WIDTH, GROUP), BF16),
            jax.ShapeDtypeStruct((1, WIDTH), F32),
        ),
        in_specs=[
            rows(WIDTH),
            rows(WIDTH),
            rows(WIDTH),
            rows(LANES),
            whole((WIDTH, LANES)),
            rows(WIDTH),
            whole((1, WIDTH)),
        ],
        out_specs=(
            rows(WIDTH),
            rows(WIDTH),
            pl.BlockSpec((WIDTH, ROWS), lambda i: (0, i)),
            whole((1, WIDTH)),
        ),
        compiler_params=params(),
    )(h, mine, other, dz, router, g, gain)


def weights_back_kernel(xnt_ref, lowt_ref, dqkv_ref, o_ref, out_ref):
    width = dqkv_ref.shape[1]
    out_ref[:, :width] = dot(xnt_ref[...], dqkv_ref[...]).astype(BF16)
    out_ref[:, width:] = dot(lowt_ref[...], o_ref[...]).astype(BF16)


def weights_back(xnt, lowt, dqkv, o):
    cols = dqkv.shape[1] + o.shape[1]
    rows = lambda width: pl.BlockSpec((ROWS, width), lambda i: (i, 0))
    return pl.pallas_call(
        weights_back_kernel,
        name="weights_back",
        grid=(WIDTH // ROWS,),
        out_shape=jax.ShapeDtypeStruct((WIDTH, cols), BF16),
        in_specs=[rows(GROUP), rows(GROUP), whole(dqkv.shape), whole(o.shape)],
        out_specs=rows(cols),
        compiler_params=params(),
    )(xnt, lowt, dqkv, o)


def input_kernel(first_ref, d_ref, w_ref, out_ref):
    out_ref[...] = dot_nt(d_ref[...], w_ref[:, : d_ref.shape[1]]).astype(out_ref.dtype)


def input_terms(first_block, dqkv, weights, dtype):
    half = GROUP // 2
    return pl.pallas_call(
        input_kernel,
        name="input_terms",
        grid_spec=pltpu.PrefetchScalarGridSpec(
            num_scalar_prefetch=1,
            grid=(half // ROWS,),
            in_specs=[
                pl.BlockSpec((ROWS, dqkv.shape[1]), lambda i, first: (i + first[0], 0)),
                pl.BlockSpec(weights.shape, lambda i, first: (0, 0)),
            ],
            out_specs=pl.BlockSpec((ROWS, WIDTH), lambda i, first: (i, 0)),
        ),
        out_shape=jax.ShapeDtypeStruct((half, WIDTH), dtype),
        compiler_params=params(),
    )(first_block, dqkv, weights)


def last_kernel(first_ref, d_ref, w_ref, other_ref, x_ref, gain_ref, dh_ref, out_ref, gain_grad_ref):
    x = x_ref[...].astype(F32)
    dxn = dot_nt(d_ref[...], w_ref[:, : d_ref.shape[1]]) + other_ref[...].astype(F32)
    scale = lax.rsqrt(jnp.mean(x * x, axis=1, keepdims=True) + EPSILON)
    gain = gain_ref[...]
    inner = jnp.mean(dxn * gain * x, axis=1, keepdims=True)
    out_ref[...] = dh_ref[...] + scale * gain * dxn - x * (scale * scale * scale) * inner
    part = jnp.sum(dxn * x * scale, axis=0, keepdims=True)
    first = pl.program_id(0) == 0
    gain_grad_ref[...] = jnp.where(first, 0.0, gain_grad_ref[...]) + part


def last(first_block, dqkv, weights, other, x, gain, dh):
    half = GROUP // 2
    local = lambda width: pl.BlockSpec((ROWS, width), lambda i, first: (i, 0))
    shifted = lambda width: pl.BlockSpec((ROWS, width), lambda i, first: (i + first[0], 0))
    return pl.pallas_call(
        last_kernel,
        name="last",
        grid_spec=pltpu.PrefetchScalarGridSpec(
            num_scalar_prefetch=1,
            grid=(half // ROWS,),
            in_specs=[
                shifted(dqkv.shape[1]),
                pl.BlockSpec(weights.shape, lambda i, first: (0, 0)),
                local(WIDTH),
                local(WIDTH),
                pl.BlockSpec((1, WIDTH), lambda i, first: (0, 0)),
                shifted(WIDTH),
            ],
            out_specs=(local(WIDTH), pl.BlockSpec((1, WIDTH), lambda i, first: (0, 0))),
        ),
        out_shape=(
            jax.ShapeDtypeStruct((half, WIDTH), F32),
            jax.ShapeDtypeStruct((1, WIDTH), F32),
        ),
        compiler_params=params(),
    )(first_block, dqkv, weights, other, x, gain, dh)


def shards(
    tokens,
    attn_gain,
    ffn_gain,
    router,
    w_query,
    key_matrix,
    value_matrix,
    w_out_t,
    w_gate,
    w_up,
    w_down_t,
    lengths,
    routes,
    priority,
    cotangent,
):
    me = lax.axis_index("tensor")
    half = tokens.shape[0]
    depth = attn_gain.shape[0]
    q_width = w_query.shape[1]
    part = w_gate.shape[2]

    def swap(v):
        return lax.ppermute(v, "tensor", [(0, 1), (1, 0)])

    def in_order(mine, other):
        return jnp.concatenate(
            [jnp.where(me == 0, mine, other), jnp.where(me == 0, other, mine)], axis=0
        )

    small = jnp.concatenate(
        [router, attn_gain[:, None], ffn_gain[:, None], jnp.zeros((depth, LANES - EXPERTS - 2), BF16)],
        axis=1,
    )
    front = jnp.concatenate([w_query, key_matrix, value_matrix, small], axis=1)
    front_full = lax.all_gather(front, "dp", axis=0, tiled=True)
    out_pair = jnp.concatenate([w_out_t, swap(w_out_t)], axis=1)
    out_full = lax.all_gather(out_pair, "dp", axis=0, tiled=True)
    gate_pair, up_pair, down_pair = (
        w.reshape(EXPERTS // 2, 2, depth, part) for w in (w_gate, w_up, w_down_t)
    )
    packed = jnp.concatenate(
        [gate_pair[:, 0], up_pair[:, 0], gate_pair[:, 1], up_pair[:, 1], down_pair[:, 0], down_pair[:, 1]],
        axis=2,
    )
    pairs = EXPERTS // 4
    experts_a = lax.all_gather(packed[:pairs], "dp", axis=1, tiled=True)
    experts_b = lax.all_gather(packed[pairs:], "dp", axis=1, tiled=True)

    x = in_order(tokens, swap(tokens))
    valid = (jnp.arange(GROUP, dtype=jnp.int32) < lengths[0]).astype(F32)[:, None]
    g = (in_order(cotangent, swap(cotangent)).astype(F32) * valid).astype(BF16)
    gt = g.T
    member_t, keep_t = route(lengths, routes, priority)
    wide = lambda v: jnp.pad(v.T, ((0, 0), (0, LANES - EXPERTS)))
    member, keep = wide(member_t), wide(keep_t)

    frequency = ROPE_BASE ** (-jnp.arange(HEAD // 2, dtype=F32) / (HEAD // 2))
    angles = jnp.arange(GROUP, dtype=F32)[:, None] * frequency[None, :]
    cos_half, sin_half = jnp.cos(angles), jnp.sin(angles)
    cos = jnp.concatenate([cos_half, cos_half], axis=1)
    sin = jnp.concatenate([-sin_half, sin_half], axis=1)

    tail = front_full[:, q_width + 2 * HEAD :]
    gain_one = tail[:, EXPERTS].astype(F32)[None, :]
    gain_two = tail[:, EXPERTS + 1].astype(F32)[None, :]
    router_wide = tail

    xnt, q, k, v = qkv(x, gain_one, front_full, cos, sin, q_width)
    mine, others, lses = [], [], []
    for i in range(2):
        o, lse = attend(i, 2, lengths, q, k, v)
        mine.append(o)
        others.append(swap(o))
        lses.append(lse)
    parts = [
        out_project(i, 2, x, mine[i], others[i], out_full, gain_two, router_wide, member, keep)
        for i in range(2)
    ]
    h, u = (jnp.concatenate([parts[0][i], parts[1][i]], axis=0) for i in range(2))
    ut = jnp.concatenate([parts[0][2], parts[1][2]], axis=1)
    gate, gates = (jnp.concatenate([parts[0][i], parts[1][i]], axis=0) for i in (3, 4))
    o_mine = jnp.concatenate(mine, axis=0)
    lse = jnp.concatenate(lses, axis=1)

    dw_a, f, du, dg = experts(0, u, g, ut, gt, experts_a, gates)
    grads_a = lax.psum_scatter(dw_a, "dp", scatter_dimension=1, tiled=True)
    dw_b, f, du, dg = experts(pairs, u, g, ut, gt, experts_b, gates, (f, du, dg))
    grads_b = lax.psum_scatter(dw_b, "dp", scatter_dimension=1, tiled=True)

    def rows_of(v, index):
        return lax.dynamic_slice_in_dim(v, index * half, half)

    f_other = swap(rows_of(f, 1 - me))
    block_out = (
        rows_of(valid, me) * (rows_of(h, me) + rows_of(f, me).astype(F32) + f_other.astype(F32))
    ).astype(BF16)

    dg_other = wide(swap(dg[:, :EXPERTS].T))
    dz, router_grad = gates_back(dg, dg_other, gate, keep, ut)
    dh, low, lowt, gain_two_grad = middle_back(h, du, swap(du), dz, router_wide, g, gain_two)
    dqkv = attend_back(lengths, low, out_full, q, k, v, lse, cos, sin)
    blocks = half // ROWS
    theirs = input_terms(((1 - me) * blocks)[None], dqkv, front_full, BF16)
    attn_grads = weights_back(xnt, lowt, dqkv, o_mine)
    input_grad, gain_one_grad = last(
        (me * blocks)[None], dqkv, front_full, swap(theirs), tokens, gain_one, dh
    )
    attn_sum = lax.psum_scatter(attn_grads, "dp", scatter_dimension=0, tiled=True)
    gain_one_grad = gain_one_grad + swap(gain_one_grad)
    small_grads = jnp.concatenate(
        [router_grad[:, :EXPERTS], gain_one_grad.T, gain_two_grad.T], axis=1
    )
    small_sum = lax.psum_scatter(small_grads, "dp", scatter_dimension=0, tiled=True)

    grads = jnp.concatenate([grads_a, grads_b], axis=0).astype(F32)
    split = [grads[:, :, i * part : (i + 1) * part] for i in range(6)]
    both = lambda a, b: jnp.stack([split[a], split[b]], axis=1).reshape(EXPERTS, depth, part)
    attn_sum = attn_sum.astype(F32)
    return (
        block_out,
        input_grad,
        small_sum[:, EXPERTS],
        small_sum[:, EXPERTS + 1],
        small_sum[:, :EXPERTS],
        attn_sum[:, :q_width],
        attn_sum[:, q_width : q_width + HEAD],
        attn_sum[:, q_width + HEAD : q_width + 2 * HEAD],
        attn_sum[:, q_width + 2 * HEAD :],
        both(0, 2),
        both(1, 3),
        both(4, 5),
    )


def solution(mesh):
    return jax.shard_map(
        shards,
        mesh=mesh,
        in_specs=(
            P(("dp", "tensor"), None),
            P("dp"),
            P("dp"),
            P("dp", None),
            P("dp", "tensor"),
            P("dp", "tensor"),
            P("dp", "tensor"),
            P("dp", "tensor"),
            P(None, "dp", "tensor"),
            P(None, "dp", "tensor"),
            P(None, "dp", "tensor"),
            P("dp"),
            P("dp", None),
            P("dp", None),
            P(("dp", "tensor"), None),
        ),
        out_specs=(
            P(("dp", "tensor"), None),
            P(("dp", "tensor"), None),
            P("dp"),
            P("dp"),
            P("dp", None),
            P("dp", "tensor"),
            P("dp", "tensor"),
            P("dp", "tensor"),
            P("dp", "tensor"),
            P(None, "dp", "tensor"),
            P(None, "dp", "tensor"),
            P(None, "dp", "tensor"),
        ),
        check_vma=False,
    )
```
